32 devices in a mesh: groups: 2 (over y), seq: 4 (over z), mp: 2 (over x), section: 2 (over core).
Axes of the slice: x: 2, y: 2, z: 4, core: 2. Of those that a mesh axis runs over, the one named last changes fastest.
Arguments:
- features: bfloat16 [16384, 128], P(('groups', 'seq', 'section')), parts along dimension 0, may hold values from -24 to 24
- flow_index: int32 [16384], P(('groups', 'seq', 'section')), parts along dimension 0, may hold values from 0 to 8191, as said below
- enc_weight: bfloat16 [128, 512], replicated, may hold values from -0.5 to 0.5
- q_weight: bfloat16 [512, 512], P(None, 'mp'), may hold values from -1 to 1
- k_weight: bfloat16 [512, 512], P(None, 'mp'), may hold values from -1 to 1
- v_weight: bfloat16 [512, 512], P(None, 'mp'), may hold values from -0.25 to 0.25
- upstream: int32 [8, 64, 4], P('mp', ('seq', 'section')), may hold values from -1 to 63, as said below
- grad_out: bfloat16 [16384, 512], P(('groups', 'seq', 'section'), 'mp'), parts along dimension 0, may hold values from -6 to 6
Outputs:
- attended: bfloat16 [16384, 512], P(('groups', 'seq', 'section'), 'mp'), parts along dimension 0
- q_grad: float32 [1024, 512], P('groups', 'mp'), parts along dimension 0
- k_grad: float32 [1024, 512], P('groups', 'mp'), parts along dimension 0
- v_grad: float32 [1024, 512], P('groups', 'mp'), parts along dimension 0
The draws below stay inside these ranges and needn't reach their ends.
There are 2 independent parts, one for each index of `groups`. The reference program is written for one: setup_inputs(seed, part) draws one part's arguments, and reference() takes and returns one part's arrays. A program takes and returns all parts, laid end to end along the dimension named above; an argument that names none is the same for every part. Nothing has to cross between parts.
Inputs may be any that keep to these rules, and one draw needn't show every extreme that they name: `flow_index`: A permutation of the points. The rows j * 128 to (j + 1) * 128 - 1 of each point shard go to flow positions j * 1024 to (j + 1) * 1024 - 1. `upstream`: entry 0 of list (h, b) is b; every other entry is -1 (unused) or a block from b + 1 to b + 8, and the used entries of a list are distinct.
All inputs are finite; a program needn't handle non-finite values.
Results may differ from the reference program's by a relative error of at most 0.025.
The reference program's roundings to bfloat16 on the way count: a program that leaves them out, or rounds other values in their place, can miss the bound.
Values may be sent and summed in bfloat16 or wider, within the bound.
A program may use at most 64 MiB of HBM per device.

```python
import jax
import jax.numpy as jnp
from jax import lax

D = 512
HEADS = 8
HD = 64
FIN = 128
BLK = 128
NB_DEV = 8
KMAX = 4
REACH = 9
SHARDS = 8
PTS_DEV = 1024
PAIR = 128
NB = 64
POINTS = 8192


def draw_features(key, part):
    drawn_values = jnp.clip(jax.random.normal(jax.random.fold_in(key, 21), (POINTS, FIN), jnp.float32), -6.0, 6.0)
    return drawn_values.astype(jnp.bfloat16)


def projection_draw(key, salt):
    base = jnp.clip(jax.random.normal(jax.random.fold_in(key, salt), (D, D), jnp.float32), -4.0, 4.0) / jnp.sqrt(jnp.float32(D))
    return base


def draw_q_weight(key, part):
    return projection_draw(key, 41).astype(jnp.bfloat16)


def draw_k_weight(key, part):
    return projection_draw(key, 42).astype(jnp.bfloat16)


def draw_flow_index(key, part):
    key_list = jax.random.split(key, SHARDS)
    slot_table = jax.vmap(lambda subkey: jax.random.permutation(subkey, PTS_DEV))(key_list)
    slot_table = slot_table.astype(jnp.int32).reshape(SHARDS, SHARDS, PAIR).transpose(1, 0, 2)
    owners = jnp.arange(SHARDS, dtype=jnp.int32)[None, :, None] * PTS_DEV
    return (slot_table + owners).reshape(POINTS)


def draw_upstream(key, part):
    pick_key = jax.random.fold_in(key, 11)
    count_key = jax.random.fold_in(key, 12)
    offsets = jnp.arange(1, REACH, dtype=jnp.int32)
    blocks = jnp.arange(NB, dtype=jnp.int32)
    random_rank = jax.random.randint(pick_key, (HEADS, NB, REACH - 1), 0, 1 << 20) * REACH + offsets
    inside = blocks[:, None] + offsets[None, :] < NB
    ranked = jnp.where(inside[None], random_rank, (1 << 20) * REACH + offsets)
    order = jnp.argsort(ranked, axis=2)[:, :, :KMAX - 1].astype(jnp.int32)
    chosen = order + 1
    valid = blocks[None, :, None] + chosen < NB
    listed = blocks[None, :, None] + chosen
    counts = jax.random.randint(count_key, (HEADS, NB, 1), 1, KMAX + 1)
    used = (jnp.arange(1, KMAX, dtype=jnp.int32)[None, None, :] < counts) & valid
    rest = jnp.where(used, listed, -1)
    leading = jnp.broadcast_to(blocks[None, :, None], (HEADS, NB, 1))
    return jnp.concatenate([leading, rest], axis=2).astype(jnp.int32)


def steps_of(key, shape, cuts, low, largest):
    level, own = 1.0, jax.random.fold_in(key, 6)
    for position, blocks in cuts:
        heights = jnp.exp(jax.random.uniform(jax.random.fold_in(own, position), (blocks,), jnp.float32, low / len(cuts), largest / len(cuts)))
        level = level * jnp.repeat(heights, shape[position] // blocks).reshape([-1 if axis == position else 1 for axis in range(len(shape))])
    return level


def noise(own_key, shape, width, most, cuts=(), kind=jnp.bfloat16):
    result = jax.random.normal(own_key, shape, jnp.float32) * width
    if len(cuts) > 0:
        result = steps_of(own_key, shape, cuts, -0.22, 0.18) * result
    return jnp.clip(result, min=-most, max=most).astype(kind)


def setup_inputs(seed: int = 0, part: int = 0) -> dict:
    seeds = jax.random.split(jax.random.key(seed), 9)
    part_keys = jax.random.split(jax.random.fold_in(seeds[8], part), 9)
    features = draw_features(jax.random.fold_in(jax.random.fold_in(seeds[8], part), 71), part)
    flow_index = draw_flow_index(jax.random.fold_in(jax.random.fold_in(seeds[8], part), 71), part)
    enc_weight = noise(seeds[2], (FIN, D), FIN ** -0.5, 0.5)
    q_weight = draw_q_weight(jax.random.fold_in(seeds[8], 71), part)
    k_weight = draw_k_weight(jax.random.fold_in(seeds[8], 71), part)
    v_weight = noise(seeds[5], (D, D), D ** -0.5, 0.25, ((1, 2),))
    upstream = draw_upstream(jax.random.fold_in(seeds[8], 71), part)
    grad_out = noise(part_keys[7], (POINTS, D), 1.0, 6.0, ((0, 8), (1, 2)))
    return dict(features=features, flow_index=flow_index, enc_weight=enc_weight, q_weight=q_weight, k_weight=k_weight, v_weight=v_weight, upstream=upstream, grad_out=grad_out)


def block_pass(inputs):
    query_blocks, grad_blocks, key_picked, value_picked, key_mask = inputs
    logit_scale_factor = 1.0 / HD ** 0.5
    query_broadened = query_blocks.astype(jnp.float32)
    gradient_broadened = grad_blocks.astype(jnp.float32)
    key_broadened = key_picked.astype(jnp.float32)
    value_broadened = value_picked.astype(jnp.float32)
    score_matrix = jnp.einsum('nfx,ntx->nft', query_broadened, key_broadened) * logit_scale_factor
    score_matrix = jnp.where(key_mask, score_matrix, -1e+30)
    shifted = jnp.exp(score_matrix - lax.optimization_barrier(jnp.max(score_matrix, axis=2, keepdims=True)))
    probability = shifted / lax.optimization_barrier(jnp.sum(shifted, axis=2, keepdims=True))
    narrow_probability = lax.optimization_barrier(probability.astype(jnp.bfloat16)).astype(jnp.float32)
    block_attended_rows = jnp.einsum('stx,sxu->stu', narrow_probability, value_broadened).astype(jnp.bfloat16)
    probability_gradient = jnp.einsum('nfx,ntx->nft', gradient_broadened, value_broadened)
    centred = probability * (probability_gradient - lax.optimization_barrier(jnp.sum(probability * probability_gradient, axis=2, keepdims=True)))
    score_gradient = lax.optimization_barrier(centred.astype(jnp.bfloat16)).astype(jnp.float32)
    query_gradient_rows = jnp.einsum('stx,sxu->stu', score_gradient, key_broadened) * logit_scale_factor
    key_gradient_rows = jnp.einsum('mcx,mcj->mxj', score_gradient, query_broadened) * logit_scale_factor
    value_gradient_rows = jnp.einsum('mcx,mcj->mxj', narrow_probability, gradient_broadened)
    return (block_attended_rows, query_gradient_rows, key_gradient_rows, value_gradient_rows)

def head_pass(inputs):
    query_head, key_head, value_head, grad_head, block_lists = inputs
    present = block_lists >= 0
    slot_index = jnp.where(present, block_lists, 0).astype(jnp.int32)
    key_picked = key_head.reshape(NB, BLK, HD)[slot_index].reshape(SHARDS, NB_DEV, KMAX * BLK, HD)
    value_picked = value_head.reshape(NB, BLK, HD)[slot_index].reshape(SHARDS, NB_DEV, KMAX * BLK, HD)
    key_mask = jnp.repeat(present, BLK, axis=1).reshape(SHARDS, NB_DEV, 1, KMAX * BLK)
    pieces = (query_head.reshape(SHARDS, NB_DEV, BLK, HD), grad_head.reshape(SHARDS, NB_DEV, BLK, HD), key_picked, value_picked, key_mask)
    attended_head, query_gradient_rows, key_pick_grads, value_pick_grads = lax.map(block_pass, pieces)
    flat_slots = slot_index.reshape(NB * KMAX)
    key_gradient_rows = jnp.zeros((NB, BLK, HD), jnp.float32).at[flat_slots].add(key_pick_grads.reshape(NB * KMAX, BLK, HD))
    value_gradient_rows = jnp.zeros((NB, BLK, HD), jnp.float32).at[flat_slots].add(value_pick_grads.reshape(NB * KMAX, BLK, HD))
    return (attended_head.reshape(POINTS, HD), query_gradient_rows.reshape(POINTS, HD).astype(jnp.bfloat16), key_gradient_rows.reshape(POINTS, HD).astype(jnp.bfloat16), value_gradient_rows.reshape(POINTS, HD).astype(jnp.bfloat16))

def split_heads(matrix):
    return matrix.reshape(POINTS, HEADS, HD).transpose(1, 0, 2)

def join_heads(stacked):
    return stacked.transpose(1, 0, 2).reshape(POINTS, D)

def reference(features, flow_index, enc_weight, q_weight, k_weight, v_weight, upstream, grad_out):
    encoded = jax.nn.gelu(jnp.dot(features, enc_weight, preferred_element_type=jnp.float32)).astype(jnp.bfloat16)
    flowed = jnp.zeros_like(encoded).at[flow_index].set(encoded)
    widened = flowed.astype(jnp.float32)
    normed = (widened * lax.rsqrt(lax.optimization_barrier(jnp.mean(widened * widened, axis=1, keepdims=True)) + 1e-05)).astype(jnp.bfloat16)
    query_rows = jnp.dot(normed, q_weight, preferred_element_type=jnp.float32).astype(jnp.bfloat16)
    key_rows = jnp.dot(normed, k_weight, preferred_element_type=jnp.float32).astype(jnp.bfloat16)
    value_rows = jnp.dot(normed, v_weight, preferred_element_type=jnp.float32).astype(jnp.bfloat16)
    results = lax.map(head_pass, (split_heads(query_rows), split_heads(key_rows), split_heads(value_rows), split_heads(grad_out), upstream))
    attended = join_heads(results[0])
    query_gradient_rows = join_heads(results[1])
    key_gradient_rows = join_heads(results[2])
    value_gradient_rows = join_heads(results[3])
    normed_t = normed.T
    q_grad = jnp.dot(normed_t, query_gradient_rows, preferred_element_type=jnp.float32)
    k_grad = jnp.dot(normed_t, key_gradient_rows, preferred_element_type=jnp.float32)
    v_grad = jnp.dot(normed_t, value_gradient_rows, preferred_element_type=jnp.float32)
    return (attended, q_grad, k_grad, v_grad)
```

```python
import functools

import jax
import jax.numpy as jnp
from jax import lax
from jax.experimental import pallas as pl
from jax.experimental.pallas import tpu as pltpu
from jax.sharding import PartitionSpec as P

NT = (((1,), (1,)), ((), ()))
RING = ("seq", "section")
CHUNK = 512


def dot(a, b):
    return jnp.dot(a, b, preferred_element_type=jnp.float32)


def layer_kernel(
    up_ref, arrived_ref, places_ref, enc_ref, wq_ref, wk_ref, wv_ref, grad_ref,
    att_ref, gq_ref, gk_ref, gv_ref,
    normed_t, kv, kv_t, pairs, dq_t, *dkv,
):
    heads, blocks, slots = len(dkv), pairs.shape[0], 4
    points, width = grad_ref.shape
    hd = width // heads
    blk = points // blocks
    peers = lax.axis_size(RING)
    shard = lax.axis_index(RING)
    wkv = jnp.concatenate(
        [w[:, h * hd : (h + 1) * hd] for h in range(heads) for w in (wk_ref, wv_ref)], axis=1
    )
    no_weight = jnp.zeros((wq_ref.shape[0], hd), wq_ref.dtype)
    wq = jnp.concatenate(
        [w for h in range(heads) for w in (wq_ref[:, h * hd : (h + 1) * hd], no_weight)], axis=1
    )
    no_grad = jnp.zeros((points, hd), grad_ref.dtype)
    for h in range(heads):
        shifted = jnp.concatenate([no_grad, grad_ref[:, h * hd : (h + 1) * hd]], axis=1)
        pairs[:, h, blk:, :] = shifted.reshape(blocks, blk, 2 * hd)
        dkv[h][...] = jnp.zeros_like(dkv[h])

    for part in range(2):
        owner = lax.rem(shard + part, peers)
        place = places_ref[part] - owner * points
        for start in range(0, points, CHUNK):
            rows = lax.broadcasted_iota(jnp.int32, (CHUNK, points), 0) + start
            take = (rows == place).astype(jnp.float32).astype(jnp.bfloat16)
            flowed = dot(take, arrived_ref[part]).astype(jnp.bfloat16)
            encoded = jax.nn.gelu(dot(flowed, enc_ref[...])).astype(jnp.bfloat16)
            wide = encoded.astype(jnp.float32)
            mean = jnp.mean(wide * wide, axis=1, keepdims=True)
            normed = (wide * lax.rsqrt(mean + 1e-05)).astype(jnp.bfloat16)
            at = part * points + start
            normed_t[:, at : at + CHUNK] = normed.T
            projected = dot(normed, wkv).astype(jnp.bfloat16)
            turned = projected.T
            for i in range(CHUNK // blk):
                kv[at // blk + i] = projected[i * blk : (i + 1) * blk]
                kv_t[at // blk + i] = turned[:, i * blk : (i + 1) * blk]
            if part == 0:
                queries = dot(normed, wq).astype(jnp.bfloat16) * jnp.bfloat16(hd**-0.5)
                for i in range(CHUNK // blk):
                    for h in range(heads):
                        pairs[start // blk + i, h, :blk, :] = queries[
                            i * blk : (i + 1) * blk, h * 2 * hd : (h + 1) * 2 * hd
                        ]

    @pl.loop(0, blocks)
    def _(b):
        attended, query_grads = [], []
        for h in range(heads):
            index, bias = [], []
            for j in range(slots):
                entry = up_ref[(h * blocks + b) * slots + j]
                index.append(jnp.where(entry >= 0, entry - shard * blocks, 0))
                bias.append(jnp.where(entry >= 0, 0.0, -1e30).astype(jnp.float32))
            cols = slice(h * 2 * hd, (h + 1) * 2 * hd)
            keys = jnp.concatenate([kv[i, :, cols] for i in index], axis=0)
            keys_t = jnp.concatenate([kv_t[i, cols, :] for i in index], axis=1)
            pair = pairs[b, h]
            both = lax.dot_general(keys, pair, NT, preferred_element_type=jnp.float32)
            score = jnp.concatenate(
                [both[j * blk : (j + 1) * blk, :blk] + bias[j] for j in range(slots)], axis=0
            )
            prob_grad = both[:, blk:]
            e = jnp.exp(score - jnp.max(score, axis=0, keepdims=True))
            prob = e * (1.0 / jnp.sum(e, axis=0, keepdims=True))
            centre = jnp.sum(prob * prob_grad, axis=0, keepdims=True)
            score_grad = prob * (prob_grad - centre)
            narrow = jnp.concatenate(
                [score_grad.astype(jnp.bfloat16), prob.astype(jnp.bfloat16)], axis=1
            )
            back = dot(narrow, pair)
            for j in range(slots):
                dkv[h][index[j]] += back[j * blk : (j + 1) * blk]
            ahead = dot(keys_t, narrow)
            query_grads.append(ahead[:hd, :blk])
            attended.append(ahead[hd:, blk:])
        rows = pl.ds(pl.multiple_of(b * blk, blk), blk)
        att_ref[rows, :] = jnp.concatenate(attended, axis=0).T.astype(jnp.bfloat16)
        dq_t[b] = jnp.concatenate(query_grads, axis=0).astype(jnp.bfloat16)

    turned = jnp.concatenate([dq_t[b] for b in range(blocks)], axis=1)
    gq_ref[...] = lax.dot_general(
        normed_t[:, :points], turned, NT, preferred_element_type=jnp.float32
    ) * (hd**-0.5)
    for h in range(0, heads, 2):
        two = jnp.concatenate(
            [dkv[h + i][...].reshape(2 * points, 2 * hd).astype(jnp.bfloat16) for i in range(2)],
            axis=1,
        )
        g = dot(normed_t[...], two)
        cols = slice(h * hd, (h + 2) * hd)
        gk_ref[:, cols] = jnp.concatenate([g[:, :hd], g[:, 2 * hd : 3 * hd]], axis=1)
        gv_ref[:, cols] = jnp.concatenate([g[:, hd : 2 * hd], g[:, 3 * hd :]], axis=1)


def body(features, flow_index, enc_weight, q_weight, k_weight, v_weight, upstream, grad_out):
    points, fin = features.shape
    peers = lax.axis_size(RING)
    heads, blocks, slots = upstream.shape
    d, width = q_weight.shape
    hd = width // heads
    blk = points // blocks
    arrived = lax.all_to_all(
        features.reshape(peers, points // peers, fin), RING, split_axis=0, concat_axis=0, tiled=True
    ).reshape(points, fin)
    places = lax.all_to_all(
        flow_index.reshape(peers, points // peers), RING, split_axis=0, concat_axis=0, tiled=True
    ).reshape(1, points)
    back = [(i, i - 1) for i in range(1, peers)]
    arrived = jnp.stack([arrived, lax.ppermute(arrived, RING, back)])
    places = jnp.stack([places, lax.ppermute(places, RING, back)])
    vmem = pl.BlockSpec(memory_space=pltpu.VMEM)
    grads = jax.ShapeDtypeStruct((d, width), jnp.float32)
    attended, gq, gk, gv = pl.pallas_call(
        layer_kernel,
        out_shape=(jax.ShapeDtypeStruct((points, width), jnp.bfloat16), grads, grads, grads),
        in_specs=[pl.BlockSpec(memory_space=pltpu.SMEM)] + [vmem] * 7,
        out_specs=(vmem,) * 4,
        scratch_shapes=[
            pltpu.VMEM((d, 2 * points), jnp.bfloat16),
            pltpu.VMEM((2 * blocks, blk, 2 * width), jnp.bfloat16),
            pltpu.VMEM((2 * blocks, 2 * width, blk), jnp.bfloat16),
            pltpu.VMEM((blocks, heads, 2 * blk, 2 * hd), jnp.bfloat16),
            pltpu.VMEM((blocks, width, blk), jnp.bfloat16),
        ]
        + [pltpu.VMEM((2 * blocks, blk, 2 * hd), jnp.float32)] * heads,
        compiler_params=pltpu.CompilerParams(vmem_limit_bytes=50 << 20),
        name="layer",
    )(
        upstream.reshape(-1), arrived, places, enc_weight, q_weight, k_weight, v_weight, grad_out
    )
    return (attended,) + lax.psum((gq, gk, gv), RING)


def solution(mesh):
    return jax.shard_map(
        body,
        mesh=mesh,
        in_specs=(
            P(("groups", "seq", "section"), None),
            P(("groups", "seq", "section")),
            P(),
            P(None, "mp"),
            P(None, "mp"),
            P(None, "mp"),
            P("mp", ("seq", "section"), None),
            P(("groups", "seq", "section"), "mp"),
        ),
        out_specs=(
            P(("groups", "seq", "section"), "mp"),
            P("groups", "mp"),
            P("groups", "mp"),
            P("groups", "mp"),
        ),
        check_vma=False,
    )
```

```python
import functools

import jax
import jax.numpy as jnp
from jax import lax
from jax.experimental import pallas as pl
from jax.experimental.pallas import tpu as pltpu
from jax.sharding import PartitionSpec as P

NT = (((1,), (1,)), ((), ()))
RING = ("seq", "section")
CHUNK = 512


def dot(a, b):
    return jnp.dot(a, b, preferred_element_type=jnp.float32)


MESH = pl.DeviceIdType.MESH
PIECES = 6


def order_kernel(
    rows_ref, index_ref, out_ref,
    got, got_index, total, mine, following, sent, landed, sent_index, landed_index, halo,
):
    peers, pair, _ = got.shape
    points = rows_ref.shape[0]
    cores = lax.axis_size("section")
    me = lax.axis_index(RING)

    def device(i):
        return {"seq": i // cores, "section": lax.rem(i, cores)}

    def send(to, frm):
        return (
            pltpu.make_async_remote_copy(
                rows_ref.at[pl.ds(pl.multiple_of(to * pair, pair), pair)], got.at[frm],
                sent.at[to], landed.at[frm], device_id=device(to), device_id_type=MESH,
            ),
            pltpu.make_async_remote_copy(
                index_ref.at[to], got_index.at[frm],
                sent_index.at[to], landed_index.at[frm], device_id=device(to), device_id_type=MESH,
            ),
        )

    def place(index, rows):
        at = lax.broadcasted_iota(jnp.int32, (points, pair), 0)
        return dot((at == index - me * points).astype(jnp.float32).astype(jnp.bfloat16), rows)

    barrier = pltpu.get_barrier_semaphore()

    @pl.loop(1, peers)
    def _(i):
        pl.semaphore_signal(
            barrier, inc=1, device_id=device(lax.rem(me + i, peers)), device_id_type=MESH
        )

    pl.semaphore_wait(barrier, peers - 1)

    @pl.loop(1, peers)
    def _(i):
        rows, index = send(lax.rem(me + i, peers), me)
        index.start()
        rows.start()

    total[...] = place(index_ref[me], rows_ref[pl.ds(pl.multiple_of(me * pair, pair), pair), :])

    @pl.loop(1, peers)
    def _(i):
        frm = lax.rem(me - i + peers, peers)
        rows, index = send(frm, frm)
        index.wait_recv()
        rows.wait_recv()
        total[...] += place(got_index[frm], got[frm])

    mine[...] = total[...].astype(jnp.bfloat16)
    before = lax.rem(me - 1 + peers, peers)
    copy = pltpu.make_async_remote_copy(
        mine, following, halo.at[0], halo.at[1], device_id=device(before), device_id_type=MESH
    )
    copy.start()
    out_ref[0] = mine[...]

    @pl.loop(1, peers)
    def _(i):
        rows, index = send(lax.rem(me + i, peers), me)
        index.wait_send()
        rows.wait_send()

    copy.wait()
    out_ref[1] = following[...]


def sum_kernel(g_ref, out_ref, beside, part, up, cross, whole, *sems):
    (
        beside_sent, beside_got, inner_sent, up_got, cross_got,
        outer_sent, outer_got, final_sent, final_got,
    ) = sems
    half = part.shape[0]
    step = half // PIECES
    chips = lax.axis_size("seq")
    z, core = lax.axis_index("seq"), lax.axis_index("section")
    base, other = core * half, (1 - core) * half
    left = z < chips // 2
    inner = jnp.where(left, z + 1, z - 1)
    outer = jnp.where(left, z - 1, z + 1)
    is_end = (z == 0) | (z == chips - 1)
    is_mid = (z == chips // 2 - 1) | (z == chips // 2)
    sibling = {"section": 1 - core}

    def at(ref, first, t):
        return ref.at[pl.ds(pl.multiple_of(first + t * step, step), step)]

    def remote(src, dst, send_sem, recv_sem, t, to):
        return pltpu.make_async_remote_copy(
            src, dst, send_sem.at[t], recv_sem.at[t], device_id=to, device_id_type=MESH
        )

    def to_sibling(t):
        return remote(at(g_ref, other, t), at(beside, 0, t), beside_sent, beside_got, t, sibling)

    def to_inner(t, dst, got):
        return remote(at(part, 0, t), at(dst, 0, t), inner_sent, got, t, {"seq": inner})

    def to_outer(t):
        return remote(at(whole, base, t), at(whole, base, t), outer_sent, outer_got, t, {"seq": outer})

    def final(t, first):
        return remote(at(whole, first, t), at(whole, first, t), final_sent, final_got, t, sibling)

    barrier = pltpu.get_barrier_semaphore()
    pl.semaphore_signal(barrier, inc=1, device_id=sibling, device_id_type=MESH)
    pl.semaphore_signal(barrier, inc=1, device_id={"seq": inner}, device_id_type=MESH)

    @pl.when(is_end)
    def _():
        pl.semaphore_wait(barrier, 2)

    @pl.when(jnp.logical_not(is_end))
    def _():
        pl.semaphore_signal(barrier, inc=1, device_id={"seq": outer}, device_id_type=MESH)
        pl.semaphore_wait(barrier, 3)

    for t in range(PIECES):
        to_sibling(t).start()

    def inward(t):
        to_sibling(t).wait_recv()
        here = at(part, 0, t)
        both = at(g_ref, base, t)[...].astype(jnp.float32) + at(beside, 0, t)[...].astype(jnp.float32)

        @pl.when(is_end)
        def _():
            here[...] = both.astype(jnp.bfloat16)

        @pl.when(jnp.logical_not(is_end))
        def _():
            to_inner(t, up, up_got).wait_recv()
            here[...] = (both + at(up, 0, t)[...].astype(jnp.float32)).astype(jnp.bfloat16)

        @pl.when(is_mid)
        def _():
            to_inner(t, cross, cross_got).start()

        @pl.when(jnp.logical_not(is_mid))
        def _():
            to_inner(t, up, up_got).start()

    def outward(t):
        @pl.when(jnp.logical_not(is_end))
        def _():
            to_outer(t).start()

        final(t, base).start()

    for t in range(PIECES + 1):
        if t < PIECES:
            inward(t)
        if t >= 1:

            @pl.when(is_mid)
            def _():
                to_inner(t - 1, cross, cross_got).wait_recv()
                at(whole, base, t - 1)[...] = (
                    at(part, 0, t - 1)[...].astype(jnp.float32)
                    + at(cross, 0, t - 1)[...].astype(jnp.float32)
                ).astype(jnp.bfloat16)
                outward(t - 1)

    for t in range(PIECES):

        @pl.when(jnp.logical_not(is_mid))
        def _():
            to_outer(t).wait_recv()
            outward(t)

    mine = pl.ds(pl.multiple_of(base, half), half)
    out_ref[mine, :] = whole[mine, :]
    for t in range(PIECES):
        final(t, other).wait_recv()
        rows = pl.ds(pl.multiple_of(other + t * step, step), step)
        out_ref[rows, :] = whole[rows, :]
    for t in range(PIECES):
        to_sibling(t).wait_send()
        to_inner(t, up, up_got).wait_send()
        final(t, base).wait_send()

        @pl.when(jnp.logical_not(is_end))
        def _():
            to_outer(t).wait_send()


def layer_kernel(
    up_ref, flowed_ref, enc_ref, wq_ref, wk_ref, wv_ref, grad_ref,
    att_ref, g_ref,
    normed_t, kv, kv_t, pairs, dq_t, *dkv,
):
    heads, blocks, slots = len(dkv), pairs.shape[0], 4
    points, width = grad_ref.shape
    hd = width // heads
    blk = points // blocks
    shard = lax.axis_index(RING)
    wkv = jnp.concatenate(
        [w[:, h * hd : (h + 1) * hd] for h in range(heads) for w in (wk_ref, wv_ref)], axis=1
    )
    no_weight = jnp.zeros((wq_ref.shape[0], hd), wq_ref.dtype)
    wq = jnp.concatenate(
        [w for h in range(heads) for w in (wq_ref[:, h * hd : (h + 1) * hd], no_weight)], axis=1
    )
    no_grad = jnp.zeros((points, hd), grad_ref.dtype)
    for h in range(heads):
        shifted = jnp.concatenate([no_grad, grad_ref[:, h * hd : (h + 1) * hd]], axis=1)
        pairs[:, h, blk:, :] = shifted.reshape(blocks, blk, 2 * hd)
        dkv[h][...] = jnp.zeros_like(dkv[h])

    for part in range(2):
        for start in range(0, points, CHUNK):
            flowed = flowed_ref[part, start : start + CHUNK, :]
            encoded = jax.nn.gelu(dot(flowed, enc_ref[...])).astype(jnp.bfloat16)
            wide = encoded.astype(jnp.float32)
            mean = jnp.mean(wide * wide, axis=1, keepdims=True)
            normed = (wide * lax.rsqrt(mean + 1e-05)).astype(jnp.bfloat16)
            at = part * points + start
            normed_t[:, at : at + CHUNK] = normed.T
            projected = dot(normed, wkv).astype(jnp.bfloat16)
            turned = projected.T
            for i in range(CHUNK // blk):
                kv[at // blk + i] = projected[i * blk : (i + 1) * blk]
                kv_t[at // blk + i] = turned[:, i * blk : (i + 1) * blk]
            if part == 0:
                queries = dot(normed, wq).astype(jnp.bfloat16) * jnp.bfloat16(hd**-0.5)
                for i in range(CHUNK // blk):
                    for h in range(heads):
                        pairs[start // blk + i, h, :blk, :] = queries[
                            i * blk : (i + 1) * blk, h * 2 * hd : (h + 1) * 2 * hd
                        ]

    @pl.loop(0, blocks)
    def _(b):
        attended, query_grads = [], []
        for h in range(heads):
            index, bias = [], []
            for j in range(slots):
                entry = up_ref[(h * blocks + b) * slots + j]
                index.append(jnp.where(entry >= 0, entry - shard * blocks, 0))
                bias.append(jnp.where(entry >= 0, 0.0, -1e30).astype(jnp.float32))
            cols = slice(h * 2 * hd, (h + 1) * 2 * hd)
            keys = jnp.concatenate([kv[i, :, cols] for i in index], axis=0)
            keys_t = jnp.concatenate([kv_t[i, cols, :] for i in index], axis=1)
            pair = pairs[b, h]
            both = lax.dot_general(keys, pair, NT, preferred_element_type=jnp.float32)
            score = jnp.concatenate(
                [both[j * blk : (j + 1) * blk, :blk] + bias[j] for j in range(slots)], axis=0
            )
            prob_grad = both[:, blk:]
            e = jnp.exp(score - jnp.max(score, axis=0, keepdims=True))
            prob = e * (1.0 / jnp.sum(e, axis=0, keepdims=True))
            centre = jnp.sum(prob * prob_grad, axis=0, keepdims=True)
            score_grad = prob * (prob_grad - centre)
            narrow = jnp.concatenate(
                [score_grad.astype(jnp.bfloat16), prob.astype(jnp.bfloat16)], axis=1
            )
            back = dot(narrow, pair)
            for j in range(slots):
                dkv[h][index[j]] += back[j * blk : (j + 1) * blk]
            ahead = dot(keys_t, narrow)
            query_grads.append(ahead[:hd, :blk])
            attended.append(ahead[hd:, blk:])
        rows = pl.ds(pl.multiple_of(b * blk, blk), blk)
        att_ref[rows, :] = jnp.concatenate(attended, axis=0).T.astype(jnp.bfloat16)
        dq_t[b] = jnp.concatenate(query_grads, axis=0).astype(jnp.bfloat16)

    turned = jnp.concatenate([dq_t[b] for b in range(blocks)], axis=1)
    d = enc_ref.shape[1]
    g_ref[:d] = (
        lax.dot_general(normed_t[:, :points], turned, NT, preferred_element_type=jnp.float32)
        * (hd**-0.5)
    ).astype(jnp.bfloat16)
    for h in range(0, heads, 2):
        two = jnp.concatenate(
            [dkv[h + i][...].reshape(2 * points, 2 * hd).astype(jnp.bfloat16) for i in range(2)],
            axis=1,
        )
        g = dot(normed_t[...], two).astype(jnp.bfloat16)
        cols = slice(h * hd, (h + 2) * hd)
        g_ref[d : 2 * d, cols] = jnp.concatenate([g[:, :hd], g[:, 2 * hd : 3 * hd]], axis=1)
        g_ref[2 * d :, cols] = jnp.concatenate([g[:, hd : 2 * hd], g[:, 3 * hd :]], axis=1)


def body(features, flow_index, enc_weight, q_weight, k_weight, v_weight, upstream, grad_out):
    points, fin = features.shape
    peers = lax.axis_size(RING)
    heads, blocks, slots = upstream.shape
    d, width = q_weight.shape
    hd = width // heads
    blk = points // blocks
    pair = points // peers
    dma = pltpu.SemaphoreType.DMA
    vmem = pl.BlockSpec(memory_space=pltpu.VMEM)
    flowed = pl.pallas_call(
        order_kernel,
        out_shape=jax.ShapeDtypeStruct((2, points, fin), features.dtype),
        in_specs=[vmem] * 2,
        out_specs=vmem,
        scratch_shapes=[
            pltpu.VMEM((peers, pair, fin), features.dtype),
            pltpu.VMEM((peers, 1, pair), jnp.int32),
            pltpu.VMEM((points, fin), jnp.float32),
            pltpu.VMEM((points, fin), features.dtype),
            pltpu.VMEM((points, fin), features.dtype),
            dma((peers,)), dma((peers,)), dma((peers,)), dma((peers,)), dma((2,)),
        ],
        compiler_params=pltpu.CompilerParams(
            collective_id=0, has_side_effects=True, vmem_limit_bytes=30 << 20
        ),
        name="order",
    )(features, flow_index.reshape(peers, 1, pair))
    attended, partial = pl.pallas_call(
        layer_kernel,
        out_shape=(jax.ShapeDtypeStruct((points, width), jnp.bfloat16), jax.ShapeDtypeStruct((3 * d, width), jnp.bfloat16)),
        in_specs=[pl.BlockSpec(memory_space=pltpu.SMEM)] + [vmem] * 6,
        out_specs=(vmem,) * 2,
        scratch_shapes=[
            pltpu.VMEM((d, 2 * points), jnp.bfloat16),
            pltpu.VMEM((2 * blocks, blk, 2 * width), jnp.bfloat16),
            pltpu.VMEM((2 * blocks, 2 * width, blk), jnp.bfloat16),
            pltpu.VMEM((blocks, heads, 2 * blk, 2 * hd), jnp.bfloat16),
            pltpu.VMEM((blocks, width, blk), jnp.bfloat16),
        ]
        + [pltpu.VMEM((2 * blocks, blk, 2 * hd), jnp.float32)] * heads,
        compiler_params=pltpu.CompilerParams(vmem_limit_bytes=50 << 20),
        name="layer",
    )(
        upstream.reshape(-1), flowed, enc_weight, q_weight, k_weight, v_weight, grad_out
    )
    half = 3 * d // 2
    summed = pl.pallas_call(
        sum_kernel,
        out_shape=jax.ShapeDtypeStruct((3 * d, width), jnp.bfloat16),
        in_specs=[vmem],
        out_specs=vmem,
        scratch_shapes=[pltpu.VMEM((half, width), jnp.bfloat16)] * 4
        + [pltpu.VMEM((3 * d, width), jnp.bfloat16)]
        + [dma((PIECES,))] * 9,
        compiler_params=pltpu.CompilerParams(
            collective_id=1, has_side_effects=True, vmem_limit_bytes=30 << 20
        ),
        name="sum",
    )(partial).astype(jnp.float32)
    return (attended, summed[:d], summed[d : 2 * d], summed[2 * d :])


def solution(mesh):
    return jax.shard_map(
        body,
        mesh=mesh,
        in_specs=(
            P(("groups", "seq", "section"), None),
            P(("groups", "seq", "section")),
            P(),
            P(None, "mp"),
            P(None, "mp"),
            P(None, "mp"),
            P("mp", ("seq", "section"), None),
            P(("groups", "seq", "section"), "mp"),
        ),
        out_specs=(
            P(("groups", "seq", "section"), "mp"),
            P("groups", "mp"),
            P("groups", "mp"),
            P("groups", "mp"),
        ),
        check_vma=False,
    )
```

```python
import functools

import jax
import jax.numpy as jnp
from jax import lax
from jax.experimental import pallas as pl
from jax.experimental.pallas import tpu as pltpu
from jax.sharding import PartitionSpec as P

NT = (((1,), (1,)), ((), ()))
RING = ("seq", "section")
CHUNK = 512


def dot(a, b):
    return jnp.dot(a, b, preferred_element_type=jnp.float32)


MESH = pl.DeviceIdType.MESH
PIECES = 6


def front_kernel(
    rows_ref, index_ref, enc_in, wq_in, wk_in, wv_in, grad_in,
    normed_t, kv, kv_t, pairs,
    got, got_index, total, mine, following, enc_ref, wq_ref, wk_ref, wv_ref, grad_ref, wkv, wq,
    sent, landed, sent_index, landed_index, halo, local,
):
    peers, pair, _ = got.shape
    points = rows_ref.shape[0]
    blocks, heads = pairs.shape[:2]
    blk, hd = points // blocks, pairs.shape[3] // 2
    cores = lax.axis_size("section")
    me = lax.axis_index(RING)
    own = pl.ds(pl.multiple_of(me * pair, pair), pair)
    loads = [
        pltpu.make_async_copy(src, dst, local.at[i])
        for i, (src, dst) in enumerate(
            (
                (rows_ref.at[own], got.at[me]),
                (index_ref.at[me], got_index.at[me]),
                (grad_in, grad_ref),
                (wk_in, wk_ref),
                (wv_in, wv_ref),
                (wq_in, wq_ref),
                (enc_in, enc_ref),
            )
        )
    ]
    for load in loads:
        load.start()

    def device(i):
        return {"seq": i // cores, "section": lax.rem(i, cores)}

    def send(to, frm):
        return (
            pltpu.make_async_remote_copy(
                rows_ref.at[pl.ds(pl.multiple_of(to * pair, pair), pair)], got.at[frm],
                sent.at[to], landed.at[frm], device_id=device(to), device_id_type=MESH,
            ),
            pltpu.make_async_remote_copy(
                index_ref.at[to], got_index.at[frm],
                sent_index.at[to], landed_index.at[frm], device_id=device(to), device_id_type=MESH,
            ),
        )

    def place(index, rows):
        at = lax.broadcasted_iota(jnp.int32, (points, pair), 0)
        return dot((at == index - me * points).astype(jnp.float32).astype(jnp.bfloat16), rows)

    barrier = pltpu.get_barrier_semaphore()

    @pl.loop(1, peers)
    def _(i):
        pl.semaphore_signal(
            barrier, inc=1, device_id=device(lax.rem(me + i, peers)), device_id_type=MESH
        )

    pl.semaphore_wait(barrier, peers - 1)

    @pl.loop(1, peers)
    def _(i):
        rows, index = send(lax.rem(me + i, peers), me)
        index.start()
        rows.start()

    for load in loads:
        load.wait()
    total[...] = place(got_index[me], got[me])
    for h in range(heads):
        one, to = slice(h * hd, (h + 1) * hd), slice(2 * h * hd, 2 * (h + 1) * hd)
        wkv[:, to] = jnp.concatenate([wk_ref[:, one], wv_ref[:, one]], axis=1)
        wq[:, to] = jnp.concatenate([wq_ref[:, one], jnp.zeros_like(wq_ref[:, one])], axis=1)
        grads = grad_ref[:, one]
        shifted = jnp.concatenate([jnp.zeros_like(grads), grads], axis=1)
        pairs[:, h, blk:, :] = shifted.reshape(blocks, blk, 2 * hd)

    @pl.loop(1, peers)
    def _(i):
        frm = lax.rem(me - i + peers, peers)
        rows, index = send(frm, frm)
        index.wait_recv()
        rows.wait_recv()
        total[...] += place(got_index[frm], got[frm])

    mine[...] = total[...].astype(jnp.bfloat16)
    before = lax.rem(me - 1 + peers, peers)
    copy = pltpu.make_async_remote_copy(
        mine, following, halo.at[0], halo.at[1], device_id=device(before), device_id_type=MESH
    )
    copy.start()

    def project(part, flowed_ref):
        for start in range(0, points, CHUNK):
            flowed = flowed_ref[start : start + CHUNK, :]
            encoded = jax.nn.gelu(dot(flowed, enc_ref[...])).astype(jnp.bfloat16)
            wide = encoded.astype(jnp.float32)
            mean = jnp.mean(wide * wide, axis=1, keepdims=True)
            normed = (wide * lax.rsqrt(mean + 1e-05)).astype(jnp.bfloat16)
            at = part * points + start
            normed_t[:, at : at + CHUNK] = normed.T
            projected = dot(normed, wkv[...]).astype(jnp.bfloat16)
            turned = projected.T
            for i in range(CHUNK // blk):
                kv[at // blk + i] = projected[i * blk : (i + 1) * blk]
                kv_t[at // blk + i] = turned[:, i * blk : (i + 1) * blk]
            if part == 0:
                queries = dot(normed, wq[...]).astype(jnp.bfloat16) * jnp.bfloat16(hd**-0.5)
                for i in range(CHUNK // blk):
                    for h in range(heads):
                        pairs[start // blk + i, h, :blk, :] = queries[
                            i * blk : (i + 1) * blk, h * 2 * hd : (h + 1) * 2 * hd
                        ]

    project(0, mine)
    copy.wait()
    project(1, following)

    @pl.loop(1, peers)
    def _(i):
        rows, index = send(lax.rem(me + i, peers), me)
        index.wait_send()
        rows.wait_send()


def sum_kernel(g_ref, out_ref, beside, part, up, cross, whole, *sems):
    (
        beside_sent, beside_got, inner_sent, up_got, cross_got,
        outer_sent, outer_got, final_sent, final_got,
    ) = sems
    half = part.shape[0]
    step = half // PIECES
    chips = lax.axis_size("seq")
    z, core = lax.axis_index("seq"), lax.axis_index("section")
    base, other = core * half, (1 - core) * half
    left = z < chips // 2
    inner = jnp.where(left, z + 1, z - 1)
    outer = jnp.where(left, z - 1, z + 1)
    is_end = (z == 0) | (z == chips - 1)
    is_mid = (z == chips // 2 - 1) | (z == chips // 2)
    sibling = {"section": 1 - core}

    def at(ref, first, t):
        return ref.at[pl.ds(pl.multiple_of(first + t * step, step), step)]

    def remote(src, dst, send_sem, recv_sem, t, to):
        return pltpu.make_async_remote_copy(
            src, dst, send_sem.at[t], recv_sem.at[t], device_id=to, device_id_type=MESH
        )

    def to_sibling(t):
        return remote(at(g_ref, other, t), at(beside, 0, t), beside_sent, beside_got, t, sibling)

    def to_inner(t, dst, got):
        return remote(at(part, 0, t), at(dst, 0, t), inner_sent, got, t, {"seq": inner})

    def to_outer(t):
        return remote(at(whole, base, t), at(whole, base, t), outer_sent, outer_got, t, {"seq": outer})

    def final(t, first):
        return remote(at(whole, first, t), at(whole, first, t), final_sent, final_got, t, sibling)

    barrier = pltpu.get_barrier_semaphore()
    pl.semaphore_signal(barrier, inc=1, device_id=sibling, device_id_type=MESH)
    pl.semaphore_signal(barrier, inc=1, device_id={"seq": inner}, device_id_type=MESH)

    @pl.when(is_end)
    def _():
        pl.semaphore_wait(barrier, 2)

    @pl.when(jnp.logical_not(is_end))
    def _():
        pl.semaphore_signal(barrier, inc=1, device_id={"seq": outer}, device_id_type=MESH)
        pl.semaphore_wait(barrier, 3)

    for t in range(PIECES):
        to_sibling(t).start()

    def inward(t):
        to_sibling(t).wait_recv()
        here = at(part, 0, t)
        both = at(g_ref, base, t)[...].astype(jnp.float32) + at(beside, 0, t)[...].astype(jnp.float32)

        @pl.when(is_end)
        def _():
            here[...] = both.astype(jnp.bfloat16)

        @pl.when(jnp.logical_not(is_end))
        def _():
            to_inner(t, up, up_got).wait_recv()
            here[...] = (both + at(up, 0, t)[...].astype(jnp.float32)).astype(jnp.bfloat16)

        @pl.when(is_mid)
        def _():
            to_inner(t, cross, cross_got).start()

        @pl.when(jnp.logical_not(is_mid))
        def _():
            to_inner(t, up, up_got).start()

    def outward(t):
        @pl.when(jnp.logical_not(is_end))
        def _():
            to_outer(t).start()

        final(t, base).start()

    for t in range(PIECES + 1):
        if t < PIECES:
            inward(t)
        if t >= 1:

            @pl.when(is_mid)
            def _():
                to_inner(t - 1, cross, cross_got).wait_recv()
                at(whole, base, t - 1)[...] = (
                    at(part, 0, t - 1)[...].astype(jnp.float32)
                    + at(cross, 0, t - 1)[...].astype(jnp.float32)
                ).astype(jnp.bfloat16)
                outward(t - 1)

    for t in range(PIECES):

        @pl.when(jnp.logical_not(is_mid))
        def _():
            to_outer(t).wait_recv()
            outward(t)

    mine = pl.ds(pl.multiple_of(base, half), half)
    out_ref[mine, :] = whole[mine, :]
    for t in range(PIECES):
        final(t, other).wait_recv()
        rows = pl.ds(pl.multiple_of(other + t * step, step), step)
        out_ref[rows, :] = whole[rows, :]
    for t in range(PIECES):
        to_sibling(t).wait_send()
        to_inner(t, up, up_got).wait_send()
        final(t, base).wait_send()

        @pl.when(jnp.logical_not(is_end))
        def _():
            to_outer(t).wait_send()


def layer_kernel(up_ref, normed_t, kv, kv_t, pairs, att_ref, g_ref, dq_t, *dkv):
    heads, blocks, slots = len(dkv), pairs.shape[0], up_ref.shape[1]
    points, width = att_ref.shape
    d = normed_t.shape[0]
    hd = width // heads
    blk = points // blocks
    shard = lax.axis_index(RING)
    for h in range(heads):
        dkv[h][...] = jnp.zeros_like(dkv[h])

    @pl.loop(0, blocks)
    def _(b):
        attended, query_grads = [], []
        for h in range(heads):
            index, bias = [], []
            for j in range(slots):
                entry = up_ref[h, j, b]
                index.append(jnp.where(entry >= 0, entry - shard * blocks, 0))
                bias.append(jnp.where(entry >= 0, 0.0, -1e30).astype(jnp.float32))
            cols = slice(h * 2 * hd, (h + 1) * 2 * hd)
            keys = jnp.concatenate([kv[i, :, cols] for i in index], axis=0)
            keys_t = jnp.concatenate([kv_t[i, cols, :] for i in index], axis=1)
            pair = pairs[b, h]
            both = lax.dot_general(keys, pair, NT, preferred_element_type=jnp.float32)
            score = jnp.concatenate(
                [both[j * blk : (j + 1) * blk, :blk] + bias[j] for j in range(slots)], axis=0
            )
            prob_grad = both[:, blk:]
            e = jnp.exp(score - jnp.max(score, axis=0, keepdims=True))
            prob = e * (1.0 / jnp.sum(e, axis=0, keepdims=True))
            centre = jnp.sum(prob * prob_grad, axis=0, keepdims=True)
            score_grad = prob * (prob_grad - centre)
            narrow = jnp.concatenate(
                [score_grad.astype(jnp.bfloat16), prob.astype(jnp.bfloat16)], axis=1
            )
            back = dot(narrow, pair)
            for j in range(slots):
                dkv[h][index[j]] += back[j * blk : (j + 1) * blk]
            ahead = dot(keys_t, narrow)
            query_grads.append(ahead[:hd, :blk])
            attended.append(ahead[hd:, blk:])
        rows = pl.ds(pl.multiple_of(b * blk, blk), blk)
        att_ref[rows, :] = jnp.concatenate(attended, axis=0).T.astype(jnp.bfloat16)
        dq_t[b] = jnp.concatenate(query_grads, axis=0).astype(jnp.bfloat16)

    turned = jnp.concatenate([dq_t[b] for b in range(blocks)], axis=1)
    g_ref[:d] = (
        lax.dot_general(normed_t[:, :points], turned, NT, preferred_element_type=jnp.float32)
        * (hd**-0.5)
    ).astype(jnp.bfloat16)
    for h in range(0, heads, 2):
        two = jnp.concatenate(
            [dkv[h + i][...].reshape(2 * points, 2 * hd).astype(jnp.bfloat16) for i in range(2)],
            axis=1,
        )
        g = dot(normed_t[...], two).astype(jnp.bfloat16)
        cols = slice(h * hd, (h + 2) * hd)
        g_ref[d : 2 * d, cols] = jnp.concatenate([g[:, :hd], g[:, 2 * hd : 3 * hd]], axis=1)
        g_ref[2 * d :, cols] = jnp.concatenate([g[:, hd : 2 * hd], g[:, 3 * hd :]], axis=1)


def body(features, flow_index, enc_weight, q_weight, k_weight, v_weight, upstream, grad_out):
    points, fin = features.shape
    peers = lax.axis_size(RING)
    heads, blocks, slots = upstream.shape
    d, width = q_weight.shape
    hd = width // heads
    blk = points // blocks
    pair = points // peers
    dma = pltpu.SemaphoreType.DMA
    vmem = pl.BlockSpec(memory_space=pltpu.VMEM)
    bf16 = jnp.bfloat16
    hbm = pl.BlockSpec(memory_space=pltpu.HBM)
    shapes = (
        (d, 2 * points), (2 * blocks, blk, 2 * width), (2 * blocks, 2 * width, blk),
        (blocks, heads, 2 * blk, 2 * hd),
    )
    middle = pl.pallas_call(
        front_kernel,
        out_shape=[jax.ShapeDtypeStruct(shape, bf16) for shape in shapes],
        in_specs=[hbm] * 7,
        out_specs=[vmem] * 4,
        scratch_shapes=[
            pltpu.VMEM((peers, pair, fin), bf16),
            pltpu.VMEM((peers, 1, pair), jnp.int32),
            pltpu.VMEM((points, fin), jnp.float32),
            pltpu.VMEM((points, fin), bf16),
            pltpu.VMEM((points, fin), bf16),
            pltpu.VMEM((fin, d), bf16),
            pltpu.VMEM((d, width), bf16),
            pltpu.VMEM((d, width), bf16),
            pltpu.VMEM((d, width), bf16),
            pltpu.VMEM((points, width), bf16),
            pltpu.VMEM((d, 2 * width), bf16),
            pltpu.VMEM((d, 2 * width), bf16),
            dma((peers,)), dma((peers,)), dma((peers,)), dma((peers,)), dma((2,)), dma((7,)),
        ],
        compiler_params=pltpu.CompilerParams(
            collective_id=0, has_side_effects=True, vmem_limit_bytes=36 << 20
        ),
        name="front",
    )(
        *(
            pltpu.with_memory_space_constraint(array, pltpu.HBM)
            for array in (
                features, flow_index.reshape(peers, 1, pair), enc_weight, q_weight, k_weight,
                v_weight, grad_out,
            )
        )
    )
    attended, partial = pl.pallas_call(
        layer_kernel,
        out_shape=(
            jax.ShapeDtypeStruct((points, width), bf16),
            jax.ShapeDtypeStruct((3 * d, width), bf16),
        ),
        in_specs=[pl.BlockSpec(memory_space=pltpu.SMEM)] + [vmem] * 4,
        out_specs=(vmem,) * 2,
        scratch_shapes=[pltpu.VMEM((blocks, width, blk), bf16)]
        + [pltpu.VMEM((2 * blocks, blk, 2 * hd), jnp.float32)] * heads,
        compiler_params=pltpu.CompilerParams(vmem_limit_bytes=36 << 20),
        name="layer",
    )(upstream.transpose(0, 2, 1), *middle)
    half = 3 * d // 2
    summed = pl.pallas_call(
        sum_kernel,
        out_shape=jax.ShapeDtypeStruct((3 * d, width), jnp.bfloat16),
        in_specs=[vmem],
        out_specs=vmem,
        scratch_shapes=[pltpu.VMEM((half, width), jnp.bfloat16)] * 4
        + [pltpu.VMEM((3 * d, width), jnp.bfloat16)]
        + [dma((PIECES,))] * 9,
        compiler_params=pltpu.CompilerParams(
            collective_id=1, has_side_effects=True, vmem_limit_bytes=30 << 20
        ),
        name="sum",
    )(partial).astype(jnp.float32)
    return (attended, summed[:d], summed[d : 2 * d], summed[2 * d :])


def solution(mesh):
    return jax.shard_map(
        body,
        mesh=mesh,
        in_specs=(
            P(("groups", "seq", "section"), None),
            P(("groups", "seq", "section")),
            P(),
            P(None, "mp"),
            P(None, "mp"),
            P(None, "mp"),
            P("mp", ("seq", "section"), None),
            P(("groups", "seq", "section"), "mp"),
        ),
        out_specs=(
            P(("groups", "seq", "section"), "mp"),
            P("groups", "mp"),
            P("groups", "mp"),
            P("groups", "mp"),
        ),
        check_vma=False,
    )
```

```python
import functools

import jax
import jax.numpy as jnp
from jax import lax
from jax.experimental import pallas as pl
from jax.experimental.pallas import tpu as pltpu
from jax.sharding import PartitionSpec as P

NT = (((1,), (1,)), ((), ()))
RING = ("seq", "section")
CHUNK = 512


def dot(a, b):
    return jnp.dot(a, b, preferred_element_type=jnp.float32)


MESH = pl.DeviceIdType.MESH
PIECES = 4


def front_kernel(
    rows_ref, index_ref, enc_in, wq_in, wk_in, wv_in, grad_in,
    normed_t, kv, kv_t, pairs,
    got, got_index, total, mine, following, enc_ref, wq_ref, wk_ref, wv_ref, grad_ref, wkv, wq,
    sent, landed, sent_index, landed_index, halo, local,
):
    peers, pair, _ = got.shape
    points = rows_ref.shape[0]
    blocks, heads = pairs.shape[:2]
    blk, hd = points // blocks, pairs.shape[3] // 2
    cores = lax.axis_size("section")
    me = lax.axis_index(RING)
    own = pl.ds(pl.multiple_of(me * pair, pair), pair)
    loads = [
        pltpu.make_async_copy(src, dst, local.at[i])
        for i, (src, dst) in enumerate(
            (
                (rows_ref.at[own], got.at[me]),
                (index_ref.at[me], got_index.at[me]),
                (grad_in, grad_ref),
                (wk_in, wk_ref),
                (wv_in, wv_ref),
                (wq_in, wq_ref),
                (enc_in, enc_ref),
            )
        )
    ]
    for load in loads:
        load.start()

    def device(i):
        return {"seq": i // cores, "section": lax.rem(i, cores)}

    def send(to, frm):
        return (
            pltpu.make_async_remote_copy(
                rows_ref.at[pl.ds(pl.multiple_of(to * pair, pair), pair)], got.at[frm],
                sent.at[to], landed.at[frm], device_id=device(to), device_id_type=MESH,
            ),
            pltpu.make_async_remote_copy(
                index_ref.at[to], got_index.at[frm],
                sent_index.at[to], landed_index.at[frm], device_id=device(to), device_id_type=MESH,
            ),
        )

    def place(index, rows):
        at = lax.broadcasted_iota(jnp.int32, (points, pair), 0)
        return dot((at == index - me * points).astype(jnp.float32).astype(jnp.bfloat16), rows)

    barrier = pltpu.get_barrier_semaphore()

    @pl.loop(1, peers)
    def _(i):
        pl.semaphore_signal(
            barrier, inc=1, device_id=device(lax.rem(me + i, peers)), device_id_type=MESH
        )

    pl.semaphore_wait(barrier, peers - 1)

    @pl.loop(1, peers)
    def _(i):
        rows, index = send(lax.rem(me + i, peers), me)
        index.start()
        rows.start()

    for load in loads:
        load.wait()
    total[...] = place(got_index[me], got[me])
    for h in range(heads):
        one, to = slice(h * hd, (h + 1) * hd), slice(2 * h * hd, 2 * (h + 1) * hd)
        wkv[:, to] = jnp.concatenate([wk_ref[:, one], wv_ref[:, one]], axis=1)
        wq[:, to] = jnp.concatenate([wq_ref[:, one], jnp.zeros_like(wq_ref[:, one])], axis=1)
        grads = grad_ref[:, one]
        shifted = jnp.concatenate([jnp.zeros_like(grads), grads], axis=1)
        pairs[:, h, blk:, :] = shifted.reshape(blocks, blk, 2 * hd)

    @pl.loop(1, peers)
    def _(i):
        frm = lax.rem(me - i + peers, peers)
        rows, index = send(frm, frm)
        index.wait_recv()
        rows.wait_recv()
        total[...] += place(got_index[frm], got[frm])

    mine[...] = total[...].astype(jnp.bfloat16)
    before = lax.rem(me - 1 + peers, peers)
    copy = pltpu.make_async_remote_copy(
        mine, following, halo.at[0], halo.at[1], device_id=device(before), device_id_type=MESH
    )
    copy.start()

    def project(part, flowed_ref):
        for start in range(0, points, CHUNK):
            flowed = flowed_ref[start : start + CHUNK, :]
            encoded = jax.nn.gelu(dot(flowed, enc_ref[...])).astype(jnp.bfloat16)
            wide = encoded.astype(jnp.float32)
            mean = jnp.mean(wide * wide, axis=1, keepdims=True)
            normed = (wide * lax.rsqrt(mean + 1e-05)).astype(jnp.bfloat16)
            at = part * points + start
            normed_t[:, at : at + CHUNK] = normed.T
            projected = dot(normed, wkv[...]).astype(jnp.bfloat16)
            turned = projected.T
            for i in range(CHUNK // blk):
                kv[at // blk + i] = projected[i * blk : (i + 1) * blk]
                kv_t[at // blk + i] = turned[:, i * blk : (i + 1) * blk]
            if part == 0:
                queries = dot(normed, wq[...]).astype(jnp.bfloat16) * jnp.bfloat16(hd**-0.5)
                for i in range(CHUNK // blk):
                    for h in range(heads):
                        pairs[start // blk + i, h, :blk, :] = queries[
                            i * blk : (i + 1) * blk, h * 2 * hd : (h + 1) * 2 * hd
                        ]

    project(0, mine)
    copy.wait()
    project(1, following)

    @pl.loop(1, peers)
    def _(i):
        rows, index = send(lax.rem(me + i, peers), me)
        index.wait_send()
        rows.wait_send()


def sum_kernel(g_ref, out_ref, beside, part, up, cross, whole, *sems):
    (
        beside_sent, beside_got, inner_sent, up_got, cross_got,
        outer_sent, outer_got, final_sent, final_got,
    ) = sems
    half = part.shape[0]
    step = half // PIECES
    chips = lax.axis_size("seq")
    z, core = lax.axis_index("seq"), lax.axis_index("section")
    base, other = core * half, (1 - core) * half
    left = z < chips // 2
    inner = jnp.where(left, z + 1, z - 1)
    outer = jnp.where(left, z - 1, z + 1)
    is_end = (z == 0) | (z == chips - 1)
    is_mid = (z == chips // 2 - 1) | (z == chips // 2)
    sibling = {"section": 1 - core}

    def at(ref, first, t):
        return ref.at[pl.ds(pl.multiple_of(first + t * step, step), step)]

    def remote(src, dst, send_sem, recv_sem, t, to):
        return pltpu.make_async_remote_copy(
            src, dst, send_sem.at[t], recv_sem.at[t], device_id=to, device_id_type=MESH
        )

    def to_sibling(t):
        return remote(at(g_ref, other, t), at(beside, 0, t), beside_sent, beside_got, t, sibling)

    def to_inner(t, dst, got):
        return remote(at(part, 0, t), at(dst, 0, t), inner_sent, got, t, {"seq": inner})

    def to_outer(t):
        return remote(at(whole, base, t), at(whole, base, t), outer_sent, outer_got, t, {"seq": outer})

    def final(t, first):
        return remote(at(whole, first, t), at(whole, first, t), final_sent, final_got, t, sibling)

    barrier = pltpu.get_barrier_semaphore()
    pl.semaphore_signal(barrier, inc=1, device_id=sibling, device_id_type=MESH)
    pl.semaphore_signal(barrier, inc=1, device_id={"seq": inner}, device_id_type=MESH)

    @pl.when(is_end)
    def _():
        pl.semaphore_wait(barrier, 2)

    @pl.when(jnp.logical_not(is_end))
    def _():
        pl.semaphore_signal(barrier, inc=1, device_id={"seq": outer}, device_id_type=MESH)
        pl.semaphore_wait(barrier, 3)

    for t in range(PIECES):
        to_sibling(t).start()

    def inward(t):
        to_sibling(t).wait_recv()
        here = at(part, 0, t)
        both = at(g_ref, base, t)[...].astype(jnp.float32) + at(beside, 0, t)[...].astype(jnp.float32)

        @pl.when(is_end)
        def _():
            here[...] = both.astype(jnp.bfloat16)

        @pl.when(jnp.logical_not(is_end))
        def _():
            to_inner(t, up, up_got).wait_recv()
            here[...] = (both + at(up, 0, t)[...].astype(jnp.float32)).astype(jnp.bfloat16)

        @pl.when(is_mid)
        def _():
            to_inner(t, cross, cross_got).start()

        @pl.when(jnp.logical_not(is_mid))
        def _():
            to_inner(t, up, up_got).start()

    def outward(t):
        @pl.when(jnp.logical_not(is_end))
        def _():
            to_outer(t).start()

        final(t, base).start()

    for t in range(PIECES + 1):
        if t < PIECES:
            inward(t)
        if t >= 1:

            @pl.when(is_mid)
            def _():
                to_inner(t - 1, cross, cross_got).wait_recv()
                at(whole, base, t - 1)[...] = (
                    at(part, 0, t - 1)[...].astype(jnp.float32)
                    + at(cross, 0, t - 1)[...].astype(jnp.float32)
                ).astype(jnp.bfloat16)
                outward(t - 1)

    for t in range(PIECES):

        @pl.when(jnp.logical_not(is_mid))
        def _():
            to_outer(t).wait_recv()
            outward(t)

    mine = pl.ds(pl.multiple_of(base, half), half)
    out_ref[mine, :] = whole[mine, :]
    for t in range(PIECES):
        final(t, other).wait_recv()
        rows = pl.ds(pl.multiple_of(other + t * step, step), step)
        out_ref[rows, :] = whole[rows, :]
    for t in range(PIECES):
        to_sibling(t).wait_send()
        to_inner(t, up, up_got).wait_send()
        final(t, base).wait_send()

        @pl.when(jnp.logical_not(is_end))
        def _():
            to_outer(t).wait_send()


def layer_kernel(up_ref, normed_t, kv, kv_t, pairs, att_ref, g_ref, dq_t, *dkv):
    heads, blocks, slots = len(dkv), pairs.shape[0], up_ref.shape[1]
    points, width = att_ref.shape
    d = normed_t.shape[0]
    hd = width // heads
    blk = points // blocks
    shard = lax.axis_index(RING)
    for h in range(heads):
        dkv[h][...] = jnp.zeros_like(dkv[h])

    @pl.loop(0, blocks, unroll=4)
    def _(b):
        attended, query_grads = [], []
        for h in range(heads):
            index, bias = [], []
            for j in range(slots):
                entry = up_ref[h, j, b]
                index.append(jnp.where(entry >= 0, entry - shard * blocks, 0))
                bias.append(jnp.where(entry >= 0, 0.0, -1e30).astype(jnp.float32))
            cols = slice(h * 2 * hd, (h + 1) * 2 * hd)
            keys = jnp.concatenate([kv[i, :, cols] for i in index], axis=0)
            keys_t = jnp.concatenate([kv_t[i, cols, :] for i in index], axis=1)
            pair = pairs[b, h]
            both = lax.dot_general(keys, pair, NT, preferred_element_type=jnp.float32)
            score = jnp.concatenate(
                [both[j * blk : (j + 1) * blk, :blk] + bias[j] for j in range(slots)], axis=0
            )
            prob_grad = both[:, blk:]
            e = jnp.exp(score - jnp.max(score, axis=0, keepdims=True))
            prob = e * (1.0 / jnp.sum(e, axis=0, keepdims=True))
            centre = jnp.sum(prob * prob_grad, axis=0, keepdims=True)
            score_grad = prob * (prob_grad - centre)
            narrow = jnp.concatenate(
                [score_grad.astype(jnp.bfloat16), prob.astype(jnp.bfloat16)], axis=1
            )
            back = dot(narrow, pair)
            for j in range(slots):
                dkv[h][index[j]] += back[j * blk : (j + 1) * blk]
            ahead = dot(keys_t, narrow)
            query_grads.append(ahead[:hd, :blk])
            attended.append(ahead[hd:, blk:])
        rows = pl.ds(pl.multiple_of(b * blk, blk), blk)
        att_ref[rows, :] = jnp.concatenate(attended, axis=0).T.astype(jnp.bfloat16)
        dq_t[b] = jnp.concatenate(query_grads, axis=0).astype(jnp.bfloat16)

    turned = jnp.concatenate([dq_t[b] for b in range(blocks)], axis=1)
    g_ref[:d] = (
        lax.dot_general(normed_t[:, :points], turned, NT, preferred_element_type=jnp.float32)
        * (hd**-0.5)
    ).astype(jnp.bfloat16)
    for h in range(0, heads, 2):
        two = jnp.concatenate(
            [dkv[h + i][...].reshape(2 * points, 2 * hd).astype(jnp.bfloat16) for i in range(2)],
            axis=1,
        )
        g = dot(normed_t[...], two).astype(jnp.bfloat16)
        cols = slice(h * hd, (h + 2) * hd)
        g_ref[d : 2 * d, cols] = jnp.concatenate([g[:, :hd], g[:, 2 * hd : 3 * hd]], axis=1)
        g_ref[2 * d :, cols] = jnp.concatenate([g[:, hd : 2 * hd], g[:, 3 * hd :]], axis=1)


def body(features, flow_index, enc_weight, q_weight, k_weight, v_weight, upstream, grad_out):
    points, fin = features.shape
    peers = lax.axis_size(RING)
    heads, blocks, slots = upstream.shape
    d, width = q_weight.shape
    hd = width // heads
    blk = points // blocks
    pair = points // peers
    dma = pltpu.SemaphoreType.DMA
    vmem = pl.BlockSpec(memory_space=pltpu.VMEM)
    bf16 = jnp.bfloat16
    hbm = pl.BlockSpec(memory_space=pltpu.HBM)
    shapes = (
        (d, 2 * points), (2 * blocks, blk, 2 * width), (2 * blocks, 2 * width, blk),
        (blocks, heads, 2 * blk, 2 * hd),
    )
    middle = pl.pallas_call(
        front_kernel,
        out_shape=[jax.ShapeDtypeStruct(shape, bf16) for shape in shapes],
        in_specs=[hbm] * 7,
        out_specs=[vmem] * 4,
        scratch_shapes=[
            pltpu.VMEM((peers, pair, fin), bf16),
            pltpu.VMEM((peers, 1, pair), jnp.int32),
            pltpu.VMEM((points, fin), jnp.float32),
            pltpu.VMEM((points, fin), bf16),
            pltpu.VMEM((points, fin), bf16),
            pltpu.VMEM((fin, d), bf16),
            pltpu.VMEM((d, width), bf16),
            pltpu.VMEM((d, width), bf16),
            pltpu.VMEM((d, width), bf16),
            pltpu.VMEM((points, width), bf16),
            pltpu.VMEM((d, 2 * width), bf16),
            pltpu.VMEM((d, 2 * width), bf16),
            dma((peers,)), dma((peers,)), dma((peers,)), dma((peers,)), dma((2,)), dma((7,)),
        ],
        compiler_params=pltpu.CompilerParams(
            collective_id=0, has_side_effects=True, vmem_limit_bytes=36 << 20
        ),
        name="front",
    )(
        *(
            pltpu.with_memory_space_constraint(array, pltpu.HBM)
            for array in (
                features, flow_index.reshape(peers, 1, pair), enc_weight, q_weight, k_weight,
                v_weight, grad_out,
            )
        )
    )
    attended, partial = pl.pallas_call(
        layer_kernel,
        out_shape=(
            jax.ShapeDtypeStruct((points, width), bf16),
            jax.ShapeDtypeStruct((3 * d, width), bf16),
        ),
        in_specs=[pl.BlockSpec(memory_space=pltpu.SMEM)] + [vmem] * 4,
        out_specs=(vmem,) * 2,
        scratch_shapes=[pltpu.VMEM((blocks, width, blk), bf16)]
        + [pltpu.VMEM((2 * blocks, blk, 2 * hd), jnp.float32)] * heads,
        compiler_params=pltpu.CompilerParams(vmem_limit_bytes=36 << 20),
        name="layer",
    )(pltpu.with_memory_space_constraint(upstream.transpose(0, 2, 1), pltpu.HBM), *middle)
    half = 3 * d // 2
    summed = pl.pallas_call(
        sum_kernel,
        out_shape=jax.ShapeDtypeStruct((3 * d, width), jnp.bfloat16),
        in_specs=[vmem],
        out_specs=vmem,
        scratch_shapes=[pltpu.VMEM((half, width), jnp.bfloat16)] * 4
        + [pltpu.VMEM((3 * d, width), jnp.bfloat16)]
        + [dma((PIECES,))] * 9,
        compiler_params=pltpu.CompilerParams(
            collective_id=1, has_side_effects=True, vmem_limit_bytes=30 << 20
        ),
        name="sum",
    )(partial).astype(jnp.float32)
    return (attended, summed[:d], summed[d : 2 * d], summed[2 * d :])


def solution(mesh):
    return jax.shard_map(
        body,
        mesh=mesh,
        in_specs=(
            P(("groups", "seq", "section"), None),
            P(("groups", "seq", "section")),
            P(),
            P(None, "mp"),
            P(None, "mp"),
            P(None, "mp"),
            P("mp", ("seq", "section"), None),
            P(("groups", "seq", "section"), "mp"),
        ),
        out_specs=(
            P(("groups", "seq", "section"), "mp"),
            P("groups", "mp"),
            P("groups", "mp"),
            P("groups", "mp"),
        ),
        check_vma=False,
    )
```
